32 devices in a mesh: row: 16 (over z, y, x), col: 2 (over core).
Axes of the slice: x: 2, y: 2, z: 4, core: 2. Of those that a mesh axis runs over, the one named last changes fastest.
Arguments:
- trailing: bfloat16 [8192, 1024], P('row', 'col'), may hold values from -6 to 6
- u_factor: bfloat16 [16, 2, 512, 256], P('row', 'col'), may hold values from -0.07861328 to 0.07861328
- w_factor: bfloat16 [16, 2, 512, 256], P('row', 'col'), may hold values from -4.1875 to 4.1875
- diag_inverse: bfloat16 [2, 512, 512], P('col'), as said below
- ranks: int32 [16, 2], P('row', 'col'), may hold values from 32 to 256, as said below
- col_rows: int32 [2], replicated, may hold values from 0 to 15, as said below
Outputs:
- updated: float32 [8192, 1024], P('row', 'col')
The draws below stay inside these ranges and needn't reach their ends.
Inputs may be any that keep to these rules, and one draw needn't show every extreme that they name: `ranks`: each tile's rank; some tile has rank 256 and some has rank 256 // 8. `col_rows`: distinct tile rows. `diag_inverse`: lower triangular, diagonal between 0.5 and 2.
All inputs are finite; a program needn't handle non-finite values.
Results may differ from the reference program's by a relative error of at most 0.0047.
Values may be sent and summed in bfloat16 or wider, within the bound.
No kernel may reach another device: no remote copies, remote signals or barrier semaphores. Data moves between devices by JAX's collectives and lax.ppermute only.
A program may use at most 64 MiB of HBM per device.

```python
import jax
import jax.numpy as jnp
from jax import lax

TILE = 512
RMAX = 256
PANELS = 2
ROWS = 16
COLS = 2


def draw_diag_inverse(key, part):
    first, second = jax.random.split(jax.random.fold_in(key, 11))
    lower = jax.random.normal(first, (PANELS, TILE, TILE), jnp.float32) / TILE ** 0.5
    lower = jnp.tril(lower, -1)
    diag_values = jnp.exp(jax.random.uniform(second, (PANELS, TILE), jnp.float32, jnp.log(0.5), jnp.log(2.0)))
    eye = jnp.eye(TILE, dtype=jnp.float32)
    return (lower + eye[None, :, :] * diag_values[:, :, None]).astype(jnp.bfloat16)


def draw_ranks(key, part):
    values = jax.random.randint(jax.random.fold_in(key, 23), (ROWS, PANELS), RMAX // 8, RMAX + 1)
    values = values.at[0, 0].set(RMAX)
    values = values.at[ROWS - 1, PANELS - 1].set(RMAX // 8)
    return values.astype(jnp.int32)


def draw_col_rows(key, part):
    inner = jax.random.permutation(jax.random.fold_in(key, 37), max(ROWS - 2, 1))[:COLS - 2].astype(jnp.int32) + 1
    ends = jnp.array([0, ROWS - 1], dtype=jnp.int32)
    chosen = jnp.concatenate([ends, inner])
    order = jax.random.permutation(jax.random.fold_in(key, 41), COLS)
    return chosen[order].astype(jnp.int32)


def steps_of(rng, extent, cuts, least, largest):
    factor_of, own = 1.0, jax.random.fold_in(rng, 6)
    for axis_at, parts in cuts:
        heights = jnp.exp(jax.random.uniform(jax.random.fold_in(own, axis_at), (parts,), jnp.float32, least / len(cuts), largest / len(cuts)))
        factor_of = factor_of * jnp.repeat(heights, extent[axis_at] // parts).reshape([-1 if axis == axis_at else 1 for axis in range(len(extent))])
    return factor_of


def noise(key, extent, scale, most, pieces=(), held_as=jnp.bfloat16):
    values = jax.random.normal(key, extent, jnp.float32) * scale
    if len(pieces) > 0:
        values = steps_of(key, extent, pieces, -0.22, 0.18) * values
    return jnp.clip(values, min=-most, max=most).astype(held_as)


def setup_inputs(seed: int = 0) -> dict:
    key_of = jax.random.split(jax.random.key(seed), 7)
    return {
        "trailing": noise(key_of[0], (ROWS * TILE, COLS * TILE), 1.0, 6.0, ((0, 16), (1, 2))),
        "u_factor": noise(key_of[1], (ROWS, PANELS, TILE, RMAX), ((RMAX * TILE ** 0.5) ** -0.5), 0.07861328, ((0, 16), (1, 2))),
        "w_factor": noise(key_of[2], (ROWS, PANELS, TILE, RMAX), 0.7, 4.1875, ((0, 16), (1, 2))),
        "diag_inverse": draw_diag_inverse(jax.random.fold_in(key_of[6], 71), 0),
        "ranks": draw_ranks(jax.random.fold_in(key_of[6], 71), 0),
        "col_rows": draw_col_rows(jax.random.fold_in(key_of[6], 71), 0),
    }


def reference(trailing, u_factor, w_factor, diag_inverse, ranks, col_rows):
    product = jnp.einsum('ktu,ikur->iktr', diag_inverse.astype(jnp.float32), w_factor.astype(jnp.float32))
    keep = jnp.arange(RMAX, dtype=jnp.int32)[None, None, :] < ranks[:, :, None]
    solved = jnp.where(keep[:, :, None, :], product.astype(jnp.bfloat16), jnp.zeros((), jnp.bfloat16))
    col_u = u_factor[col_rows].astype(jnp.float32)
    col_v = solved[col_rows].astype(jnp.float32)
    tiles = trailing.reshape(ROWS, TILE, COLS, TILE)

    def one_row(items):
        u_row, v_row, c_row = items
        core = jnp.einsum('ktr,ckts->ckrs', v_row.astype(jnp.float32), col_v).astype(jnp.bfloat16)
        mixed = jnp.einsum('ktr,ckrs->ckts', u_row.astype(jnp.float32), core.astype(jnp.float32)).astype(jnp.bfloat16)
        change = jnp.einsum('ckts,ckus->tcu', mixed.astype(jnp.float32), col_u)
        return c_row.astype(jnp.float32) - change

    result = lax.map(one_row, (u_factor, solved, tiles))
    return result.reshape(ROWS * TILE, COLS * TILE)
```

```python
import jax
import jax.numpy as jnp
from jax import lax
from jax.sharding import PartitionSpec as P

SPLIT = 2


def bit(value, at):
    return (value >> at) & 1


class Route:
    def __init__(self, rows, cols):
        bits = rows.bit_length() - 1
        low, high = list(range(SPLIT)), list(range(SPLIT, bits))
        self.orders = (low + high, low[::-1] + high[::-1])
        self.rows, self.cols, self.steps = rows, cols, bits
        self.me = lax.axis_index("row")
        self.odd = (lax.axis_index("col") & 1) == 1

    def of(self, row, step):
        even, odd = (bit(row, order[step]) for order in self.orders)
        return jnp.where(self.odd, odd, even)

    def cross(self, block, step):
        pairs = [
            (i * self.cols + c, (i ^ (1 << self.orders[c & 1][step])) * self.cols + c)
            for i in range(self.rows)
            for c in range(self.cols)
        ]
        return lax.ppermute(block, ("row", "col"), pairs)


def swap_cols(block):
    return lax.ppermute(block, "col", [(0, 1), (1, 0)])


def own_columns(slots, cols, col):
    if cols == 2:
        mine = jnp.where(col == 0, slots[0], slots[1])
        other = jnp.where(col == 0, slots[1], slots[0])
        return [mine, swap_cols(other)]
    moved = lax.all_to_all(jnp.stack(slots), "col", 0, 0, tiled=True)
    return [lax.dynamic_index_in_dim(moved, (col + k) % cols, 0, False) for k in range(cols)]


def all_panels(block, cols, col):
    if cols == 2:
        return [block, swap_cols(block)]
    moved = lax.all_gather(block, "col")
    return [lax.dynamic_index_in_dim(moved, (col + k) % cols, 0, False) for k in range(cols)]


def paired(block, route, roots, col):
    cols = route.cols
    height = block.shape[-2] // 4
    part = [
        [block[..., (2 * x + y) * height : (2 * x + y + 1) * height, :] for y in range(2)]
        for x in range(2)
    ]
    part = [[jnp.where(route.odd, part[y][x], part[x][y]) for y in range(2)] for x in range(2)]
    a, b = route.of(route.me, 0) == 1, route.of(route.me, 1) == 1
    near = [
        [route.of(root, step) == route.of(route.me, step) for step in range(route.steps)]
        for root in roots
    ]
    kept = jnp.stack([jnp.where(a, part[1][y], part[0][y]) for y in range(2)])
    sent = jnp.stack([jnp.where(a, part[0][y], part[1][y]) for y in range(2)])
    came = route.cross(sent, 0)
    slots = [jnp.where(n[0], kept, came) for n in near]
    kept = [jnp.where(b, s[1], s[0]) for s in slots]
    came = route.cross(jnp.stack([jnp.where(b, s[0], s[1]) for s in slots]), 1)
    slots = [jnp.where(n[1], k, came[c]) for c, (n, k) in enumerate(zip(near, kept))]
    for step in range(SPLIT, route.steps):
        came = route.cross(jnp.stack(slots), step)
        slots = [jnp.where(n[step], s, came[c]) for c, (n, s) in enumerate(zip(near, slots))]
    held = jnp.stack(own_columns(slots, cols, col))
    came = route.cross(held, 1)
    pair = jnp.stack([jnp.where(b, came, held), jnp.where(b, held, came)])
    came = route.cross(pair, 0)
    whole = [jnp.where(a, came, pair), jnp.where(a, pair, came)]
    whole = [[jnp.where(route.odd, whole[y][x], whole[x][y]) for y in range(2)] for x in range(2)]
    return jnp.concatenate([whole[x][y] for x in range(2) for y in range(2)], axis=-2)


def local(cols, rows, trailing, u_factor, w_factor, diag_inverse, ranks, col_rows):
    rank_max = w_factor.shape[3]
    col = lax.axis_index("col")
    route = Route(rows, cols)
    roots = [col_rows[c] for c in range(cols)]
    product = jnp.dot(diag_inverse[0], w_factor[0, 0], preferred_element_type=jnp.float32)
    keep = jnp.arange(rank_max, dtype=jnp.int32) < ranks[0, 0]
    solved = jnp.where(keep[None, :], product.astype(jnp.bfloat16), jnp.zeros((), jnp.bfloat16))
    block = jnp.stack([u_factor[0, 0], solved])
    row = jnp.stack(all_panels(block, cols, col))
    column = paired(block, route, roots, col)
    core = jnp.einsum(
        "ktr,kts->krs", row[:, 1], column[:, 1], preferred_element_type=jnp.float32
    ).astype(jnp.bfloat16)
    mixed = jnp.einsum("ktr,krs->kts", row[:, 0], core, preferred_element_type=jnp.float32)
    mixed = mixed.astype(jnp.bfloat16)
    change = jnp.einsum("kts,kus->tu", mixed, column[:, 0], preferred_element_type=jnp.float32)
    return trailing.astype(jnp.float32) - change


def solution(mesh):
    placed = (
        P("row", "col"),
        P("row", "col", None, None),
        P("row", "col", None, None),
        P("col", None, None),
        P("row", "col"),
        P(),
    )

    def step(*args):
        return local(mesh.shape["col"], mesh.shape["row"], *args)

    return jax.shard_map(
        step, mesh=mesh, in_specs=placed, out_specs=P("row", "col"), check_vma=False
    )
```

```python
import functools

import jax
import jax.numpy as jnp
from jax import lax
from jax.sharding import PartitionSpec as P

LOW = 2
FAN = ((1, 2), (2, 1), (3, 3))


def after(value, earlier):
    return lax.optimization_barrier((value, earlier))[0]


def swap_cols(block):
    return lax.ppermute(block, "col", [(0, 1), (1, 0)])


def all_panels(block, cols, col):
    if cols == 2:
        return jnp.stack([block, swap_cols(block)])
    return jnp.roll(lax.all_gather(block, "col"), -col, axis=0)


class Paths:
    def __init__(self, rows, cols, col_rows, width):
        self.rows, self.cols = rows, cols
        self.row, self.col = lax.axis_index("row"), lax.axis_index("col")
        self.odd = (self.col & 1) == 1
        self.place = self.row & ((1 << LOW) - 1)
        self.apart = jnp.broadcast_to((col_rows ^ self.row)[:, None], (cols, width))
        high = list(range(LOW, rows.bit_length() - 1))
        self.high = [(1 << even, 1 << odd) for even, odd in zip(high, high[::-1])]

    def of(self, pair):
        return jnp.where(self.odd, pair[1], pair[0])

    def cross(self, block, masks):
        rows, cols = range(self.rows), range(self.cols)
        pairs = [(i * self.cols + c, (i ^ masks[c & 1]) * self.cols + c) for i in rows for c in cols]
        return lax.ppermute(block, ("row", "col"), pairs)

    def scatter_start(self, block):
        height, width = block.shape
        parts = block.reshape(1 << LOW, height >> LOW, width)
        part = functools.partial(lax.dynamic_index_in_dim, parts, axis=0, keepdims=False)
        sent = [part(self.place ^ self.of(masks)) for masks in FAN]
        return part(self.place), [self.cross(block, masks) for block, masks in zip(sent, FAN)], sent

    def scatter_end(self, slots, came):
        low = (self.apart & ((1 << LOW) - 1))[:, None, :]
        for masks, block in zip(FAN, came):
            slots = jnp.where(low == self.of(masks), block, slots)
        return slots

    def spread(self, slots, came, step):
        mine = (jnp.arange(self.cols) == self.col)[:, None]
        apart = jnp.sum(jnp.where(mine, self.apart, 0), axis=0)
        return jnp.where((apart & self.of(self.high[step])) == 0, slots, came)

    def own_columns(self, slots):
        if self.cols == 2:
            mine = jnp.where(self.col == 0, slots[0], slots[1])
            other = jnp.where(self.col == 0, slots[1], slots[0])
            return jnp.stack([mine, swap_cols(other)])
        return jnp.roll(lax.all_to_all(slots, "col", 0, 0, tiled=True), -self.col, axis=0)

    def gather_start(self, held):
        return [held, *(self.cross(held, masks) for masks in FAN)]

    def gather_end(self, parts):
        masks = [self.of(masks) for masks in FAN]
        whole = []
        for q in range(1 << LOW):
            part = parts[0]
            for mask, came in zip(masks, parts[1:]):
                part = jnp.where((self.place ^ q) == mask, came, part)
            whole.append(part)
        return jnp.concatenate(whole, axis=1)


def local(cols, rows, trailing, u_factor, w_factor, diag_inverse, ranks, col_rows):
    rank_max = w_factor.shape[3]
    col = lax.axis_index("col")
    left, inverse = u_factor[0, 0], diag_inverse[0]
    keep = jnp.arange(rank_max, dtype=jnp.int32) < ranks[0, 0]
    right = jnp.where(keep[None, :], w_factor[0, 0], jnp.zeros((), jnp.bfloat16))
    first, second = (Paths(rows, cols, c, rank_max) for c in (col_rows, after(col_rows, left)))
    one, came_one, _ = first.scatter_start(right)
    two, came_two, sent = second.scatter_start(left)

    own = all_panels(after(jnp.stack([right, left]), sent), cols, col)
    inverse = all_panels(after(inverse, sent), cols, col)
    right, left = own[:, 0], own[:, 1]
    solve = functools.partial(jnp.einsum, "ktu,kur->ktr", preferred_element_type=jnp.float32)
    solved = solve(inverse, right).astype(jnp.bfloat16)

    one = first.own_columns(first.scatter_end(one, after(came_one, sent)))
    came_one = first.cross(one, first.high[0])
    two = second.own_columns(second.scatter_end(two, after(came_two, one)))
    came_two = second.cross(two, second.high[0])
    last = len(first.high) - 1
    for step in range(last):
        one = first.spread(one, after(came_one, two), step)
        came_one = first.cross(one, first.high[step + 1])
        two = second.spread(two, after(came_two, one), step)
        came_two = second.cross(two, second.high[step + 1])
    one = first.spread(one, after(came_one, (two, solved)), last)
    parts_one = first.gather_start(one)
    two = second.spread(two, after(came_two, parts_one[1]), last)
    parts_two = second.gather_start(two)

    right_col = first.gather_end([after(part, two) for part in parts_one])
    solved_col = solve(inverse, right_col).astype(jnp.bfloat16)
    core = jnp.einsum("ktr,kts->krs", solved, solved_col, preferred_element_type=jnp.float32)
    core = core.astype(jnp.bfloat16)
    mixed = jnp.einsum("ktr,krs->kts", left, core, preferred_element_type=jnp.float32)
    mixed = mixed.astype(jnp.bfloat16)
    left_col = second.gather_end([after(part, mixed) for part in parts_two])
    change = jnp.einsum("kts,kus->tu", mixed, left_col, preferred_element_type=jnp.float32)
    return trailing.astype(jnp.float32) - change


def solution(mesh):
    placed = (
        P("row", "col"),
        P("row", "col", None, None),
        P("row", "col", None, None),
        P("col", None, None),
        P("row", "col"),
        P(),
    )
    step = functools.partial(local, mesh.shape["col"], mesh.shape["row"])
    return jax.shard_map(
        step, mesh=mesh, in_specs=placed, out_specs=P("row", "col"), check_vma=False
    )
```

```python
import functools

import jax
import jax.numpy as jnp
from jax import lax
from jax.sharding import PartitionSpec as P

LOW = 2
FAN = ((1, 1), (2, 2), (3, 3))
BACK = ((1, 2), (2, 1), (3, 3))


def after(value, earlier):
    return lax.optimization_barrier((value, earlier))[0]


def swap_cols(block):
    return lax.ppermute(block, "col", [(0, 1), (1, 0)])


def all_panels(block, cols, col):
    if cols == 2:
        return jnp.stack([block, swap_cols(block)])
    return jnp.roll(lax.all_gather(block, "col"), -col, axis=0)


class Paths:
    def __init__(self, rows, cols, col_rows, width):
        self.rows, self.cols = rows, cols
        self.row, self.col = lax.axis_index("row"), lax.axis_index("col")
        self.odd = (self.col & 1) == 1
        self.place = self.row & ((1 << LOW) - 1)
        self.apart = jnp.broadcast_to((col_rows ^ self.row)[:, None], (cols, width))
        high = list(range(LOW, rows.bit_length() - 1))
        self.high = [(1 << even, 1 << odd) for even, odd in zip(high, high[::-1])]

    def of(self, pair):
        return jnp.where(self.odd, pair[1], pair[0])

    def cross(self, block, masks):
        rows, cols = range(self.rows), range(self.cols)
        pairs = [(i * self.cols + c, (i ^ masks[c & 1]) * self.cols + c) for i in rows for c in cols]
        return lax.ppermute(block, ("row", "col"), pairs)

    def scatter_start(self, block):
        n, height, width = block.shape
        parts = block.reshape(n, 1 << LOW, height >> LOW, width)
        part = functools.partial(lax.dynamic_index_in_dim, parts, axis=1, keepdims=False)
        sent = [part(self.place ^ self.of(masks)) for masks in FAN]
        return part(self.place), [self.cross(block, masks) for block, masks in zip(sent, FAN)], sent

    def scatter_end(self, slots, came):
        low = (self.apart & ((1 << LOW) - 1))[:, None, None, :]
        for masks, block in zip(FAN, came):
            slots = jnp.where(low == self.of(masks), block, slots)
        return slots

    def spread(self, slots, came, step):
        mine = (jnp.arange(self.cols) == self.col)[:, None]
        apart = jnp.sum(jnp.where(mine, self.apart, 0), axis=0)
        return jnp.where((apart & self.of(self.high[step])) == 0, slots, came)

    def own_columns(self, slots):
        if self.cols == 2:
            mine = jnp.where(self.col == 0, slots[0], slots[1])
            other = jnp.where(self.col == 0, slots[1], slots[0])
            return jnp.stack([mine, swap_cols(other)])
        return jnp.roll(lax.all_to_all(slots, "col", 0, 0, tiled=True), -self.col, axis=0)

    def gather_start(self, held):
        return [held, *(self.cross(held, masks) for masks in BACK)]

    def gather_end(self, parts):
        masks = [self.of(masks) for masks in BACK]
        whole = []
        for q in range(1 << LOW):
            part = parts[0]
            for mask, came in zip(masks, parts[1:]):
                part = jnp.where((self.place ^ q) == mask, came, part)
            whole.append(part)
        return jnp.concatenate(whole, axis=1)


def local(cols, rows, trailing, u_factor, w_factor, diag_inverse, ranks, col_rows):
    rank_max = w_factor.shape[3]
    col = lax.axis_index("col")
    left, inverse = u_factor[0, 0], diag_inverse[0]
    keep = jnp.arange(rank_max, dtype=jnp.int32) < ranks[0, 0]
    right = jnp.where(keep[None, :], w_factor[0, 0], jnp.zeros((), jnp.bfloat16))
    first, second = (Paths(rows, cols, c, rank_max) for c in (col_rows, after(col_rows, left)))
    both = jnp.stack([right, left])
    slots, came, sent = first.scatter_start(both)

    own = all_panels(after(both, sent), cols, col)
    inverse = all_panels(after(inverse, sent), cols, col)
    right, left = own[:, 0], own[:, 1]
    solve = functools.partial(jnp.einsum, "ktu,kur->ktr", preferred_element_type=jnp.float32)
    solved = solve(inverse, right).astype(jnp.bfloat16)
    base = trailing.astype(jnp.float32)

    both = first.own_columns(first.scatter_end(slots, came))
    one, two = both[:, 0], both[:, 1]
    came_one = first.cross(one, first.high[0])
    came_two = second.cross(two, second.high[0])
    last = len(first.high) - 1
    for step in range(last):
        one = first.spread(one, after(came_one, two), step)
        came_one = first.cross(one, first.high[step + 1])
        two = second.spread(two, after(came_two, one), step)
        came_two = second.cross(two, second.high[step + 1])
    one = first.spread(one, after(came_one, (two, solved, base)), last)
    parts_one = first.gather_start(one)
    two = second.spread(two, after(came_two, one), last)
    parts_two = second.gather_start(two)

    right_col = first.gather_end([after(part, two) for part in parts_one])
    solved_col = solve(inverse, right_col).astype(jnp.bfloat16)
    core = jnp.einsum("ktr,kts->krs", solved, solved_col, preferred_element_type=jnp.float32)
    core = core.astype(jnp.bfloat16)
    mixed = jnp.einsum("ktr,krs->kts", left, core, preferred_element_type=jnp.float32)
    mixed = mixed.astype(jnp.bfloat16)
    left_col = second.gather_end([after(part, mixed) for part in parts_two])
    change = jnp.einsum("kts,kus->tu", mixed, left_col, preferred_element_type=jnp.float32)
    return base - change


def solution(mesh):
    placed = (
        P("row", "col"),
        P("row", "col", None, None),
        P("row", "col", None, None),
        P("col", None, None),
        P("row", "col"),
        P(),
    )
    step = functools.partial(local, mesh.shape["col"], mesh.shape["row"])
    return jax.shard_map(
        step, mesh=mesh, in_specs=placed, out_specs=P("row", "col"), check_vma=False
    )
```

```python
import functools

import jax
import jax.numpy as jnp
from jax import lax
from jax.sharding import PartitionSpec as P

LOW = 2
FAN = ((1, 1), (2, 2), (3, 3))
BACK = ((2, 2), (1, 1), (3, 3))


def after(value, earlier):
    return lax.optimization_barrier((value, earlier))[0]


def swap_cols(block):
    return lax.ppermute(block, "col", [(0, 1), (1, 0)])


def all_panels(block, cols, col):
    if cols == 2:
        return jnp.stack([block, swap_cols(block)])
    return jnp.roll(lax.all_gather(block, "col"), -col, axis=0)


class Paths:
    def __init__(self, rows, cols, col_rows, width):
        self.rows, self.cols = rows, cols
        self.row, self.col = lax.axis_index("row"), lax.axis_index("col")
        self.odd = (self.col & 1) == 1
        self.place = self.row & ((1 << LOW) - 1)
        self.apart = jnp.broadcast_to((col_rows ^ self.row)[:, None], (cols, width))
        high = list(range(LOW, rows.bit_length() - 1))
        self.high = [(1 << even, 1 << odd) for even, odd in zip(high, high[::-1])]

    def of(self, pair):
        return jnp.where(self.odd, pair[1], pair[0])

    def cross(self, block, masks):
        rows, cols = range(self.rows), range(self.cols)
        pairs = [(i * self.cols + c, (i ^ masks[c & 1]) * self.cols + c) for i in rows for c in cols]
        return lax.ppermute(block, ("row", "col"), pairs)

    def scatter_start(self, block):
        n, height, width = block.shape
        parts = block.reshape(n, 1 << LOW, height >> LOW, width)
        part = functools.partial(lax.dynamic_index_in_dim, parts, axis=1, keepdims=False)
        sent = [part(self.place ^ self.of(masks)) for masks in FAN]
        return part(self.place), [self.cross(block, masks) for block, masks in zip(sent, FAN)], sent

    def scatter_end(self, slots, came):
        low = (self.apart & ((1 << LOW) - 1))[:, None, None, :]
        for masks, block in zip(FAN, came):
            slots = jnp.where(low == self.of(masks), block, slots)
        return slots

    def spread(self, slots, came, step):
        mine = (jnp.arange(self.cols) == self.col)[:, None]
        apart = jnp.sum(jnp.where(mine, self.apart, 0), axis=0)
        return jnp.where((apart & self.of(self.high[step])) == 0, slots, came)

    def own_columns(self, slots):
        if self.cols == 2:
            mine = jnp.where(self.col == 0, slots[0], slots[1])
            other = jnp.where(self.col == 0, slots[1], slots[0])
            return jnp.stack([mine, swap_cols(other)])
        return jnp.roll(lax.all_to_all(slots, "col", 0, 0, tiled=True), -self.col, axis=0)

    def gather_start(self, held):
        return [held, *(self.cross(held, masks) for masks in BACK)]

    def gather_end(self, parts):
        masks = [self.of(masks) for masks in BACK]
        whole = []
        for q in range(1 << LOW):
            part = parts[0]
            for mask, came in zip(masks, parts[1:]):
                part = jnp.where((self.place ^ q) == mask, came, part)
            whole.append(part)
        return jnp.concatenate(whole, axis=1)


def local(cols, rows, trailing, u_factor, w_factor, diag_inverse, ranks, col_rows):
    rank_max = w_factor.shape[3]
    col = lax.axis_index("col")
    left, inverse = u_factor[0, 0], diag_inverse[0]
    keep = jnp.arange(rank_max, dtype=jnp.int32) < ranks[0, 0]
    right = jnp.where(keep[None, :], w_factor[0, 0], jnp.zeros((), jnp.bfloat16))
    first, second = (Paths(rows, cols, c, rank_max) for c in (col_rows, after(col_rows, left)))
    both = jnp.stack([right, left])
    slots, came, sent = first.scatter_start(both)

    own = all_panels(both, cols, col)
    inverse = all_panels(after(inverse, own), cols, col)
    right, left = own[:, 0], own[:, 1]
    solve = functools.partial(jnp.einsum, "ktu,kur->ktr", preferred_element_type=jnp.float32)
    solved = solve(inverse, right).astype(jnp.bfloat16)
    base = trailing.astype(jnp.float32)

    both = first.own_columns(first.scatter_end(slots, came))
    one, two = both[:, 0], both[:, 1]
    came_one = first.cross(one, first.high[0])
    came_two = second.cross(two, second.high[0])
    last = len(first.high) - 1
    for step in range(last):
        one = first.spread(one, after(came_one, two), step)
        came_one = first.cross(one, first.high[step + 1])
        two = second.spread(two, after(came_two, one), step)
        came_two = second.cross(two, second.high[step + 1])
    one = first.spread(one, after(came_one, (two, base)), last)
    parts_one = first.gather_start(one)
    two = second.spread(two, after(came_two, (one, solved)), last)
    parts_two = second.gather_start(two)

    right_col = first.gather_end(parts_one)
    solved_col = solve(inverse, right_col).astype(jnp.bfloat16)
    core = jnp.einsum("ktr,kts->krs", solved, solved_col, preferred_element_type=jnp.float32)
    core = core.astype(jnp.bfloat16)
    mixed = jnp.einsum("ktr,krs->kts", left, core, preferred_element_type=jnp.float32)
    mixed = mixed.astype(jnp.bfloat16)
    left_col = second.gather_end([after(part, mixed) for part in parts_two])
    change = jnp.einsum("kts,kus->tu", mixed, left_col, preferred_element_type=jnp.float32)
    return base - change


def solution(mesh):
    placed = (
        P("row", "col"),
        P("row", "col", None, None),
        P("row", "col", None, None),
        P("col", None, None),
        P("row", "col"),
        P(),
    )
    step = functools.partial(local, mesh.shape["col"], mesh.shape["row"])
    return jax.shard_map(
        step, mesh=mesh, in_specs=placed, out_specs=P("row", "col"), check_vma=False
    )
```

```python
import functools

import jax
import jax.numpy as jnp
from jax import lax
from jax.sharding import PartitionSpec as P

LOW = 2
FAN = ((1, 1), (2, 2), (3, 3))
BACK = ((2, 2), (1, 1), (3, 3))


def after(value, earlier):
    return lax.optimization_barrier((value, earlier))[0]


def swap_cols(block):
    return lax.ppermute(block, "col", [(0, 1), (1, 0)])


def all_panels(block, cols, col):
    if cols == 2:
        return jnp.stack([block, swap_cols(block)])
    return jnp.roll(lax.all_gather(block, "col"), -col, axis=0)


class Paths:
    def __init__(self, rows, cols, col_rows, width):
        self.rows, self.cols = rows, cols
        self.row, self.col = lax.axis_index("row"), lax.axis_index("col")
        self.odd = (self.col & 1) == 1
        self.place = self.row & ((1 << LOW) - 1)
        self.apart = jnp.broadcast_to((col_rows ^ self.row)[:, None], (cols, width))
        high = list(range(LOW, rows.bit_length() - 1))
        self.high = [(1 << even, 1 << odd) for even, odd in zip(high, high[::-1])]

    def of(self, pair):
        return jnp.where(self.odd, pair[1], pair[0])

    def cross(self, block, masks):
        rows, cols = range(self.rows), range(self.cols)
        pairs = [(i * self.cols + c, (i ^ masks[c & 1]) * self.cols + c) for i in rows for c in cols]
        return lax.ppermute(block, ("row", "col"), pairs)

    def scatter_start(self, block):
        n, height, width = block.shape
        parts = block.reshape(n, 1 << LOW, height >> LOW, width)
        part = functools.partial(lax.dynamic_index_in_dim, parts, axis=1, keepdims=False)
        sent = [part(self.place ^ self.of(masks)) for masks in FAN]
        return part(self.place), [self.cross(block, masks) for block, masks in zip(sent, FAN)], sent

    def scatter_end(self, slots, came):
        low = (self.apart & ((1 << LOW) - 1))[:, None, None, :]
        for masks, block in zip(FAN, came):
            slots = jnp.where(low == self.of(masks), block, slots)
        return slots

    def spread(self, slots, came, step):
        mine = (jnp.arange(self.cols) == self.col)[:, None]
        apart = jnp.sum(jnp.where(mine, self.apart, 0), axis=0)
        return jnp.where((apart & self.of(self.high[step])) == 0, slots, came)

    def own_columns(self, slots):
        if self.cols == 2:
            mine = jnp.where(self.col == 0, slots[0], slots[1])
            other = jnp.where(self.col == 0, slots[1], slots[0])
            return jnp.stack([mine, swap_cols(other)])
        return jnp.roll(lax.all_to_all(slots, "col", 0, 0, tiled=True), -self.col, axis=0)

    def gather_start(self, held):
        return [held, *(self.cross(held, masks) for masks in BACK)]

    def gather_end(self, parts):
        masks = [self.of(masks) for masks in BACK]
        whole = []
        for q in range(1 << LOW):
            part = parts[0]
            for mask, came in zip(masks, parts[1:]):
                part = jnp.where((self.place ^ q) == mask, came, part)
            whole.append(part)
        return jnp.concatenate(whole, axis=1)


def local(cols, rows, trailing, u_factor, w_factor, diag_inverse, ranks, col_rows):
    rank_max = w_factor.shape[3]
    col = lax.axis_index("col")
    left, inverse = u_factor[0, 0], diag_inverse[0]
    keep = jnp.arange(rank_max, dtype=jnp.int32) < ranks[0, 0]
    right = jnp.where(keep[None, :], w_factor[0, 0], jnp.zeros((), jnp.bfloat16))
    first, second = (Paths(rows, cols, c, rank_max) for c in (col_rows, after(col_rows, left)))
    both = jnp.stack([right, left])
    slots, came, sent = first.scatter_start(both)

    own = all_panels(both, cols, col)
    inverse = all_panels(after(inverse, own), cols, col)
    right, left = own[:, 0], own[:, 1]
    solve = functools.partial(jnp.einsum, "ktu,kur->ktr", preferred_element_type=jnp.float32)
    solved = solve(inverse, right).astype(jnp.bfloat16)
    base = trailing.astype(jnp.float32)

    both = first.own_columns(first.scatter_end(slots, came))
    one, two = both[:, 0], both[:, 1]
    came_one = first.cross(one, first.high[0])
    came_two = second.cross(two, second.high[0])
    last = len(first.high) - 1
    for step in range(last):
        one = first.spread(one, came_one, step)
        came_one = first.cross(one, first.high[step + 1])
        two = second.spread(two, after(came_two, one), step)
        came_two = second.cross(two, second.high[step + 1])
    one = first.spread(one, after(came_one, two), last)
    parts_one = first.gather_start(one)
    two = second.spread(two, after(came_two, (one, solved, base)), last)
    parts_two = second.gather_start(two)

    right_col = first.gather_end(parts_one)
    solved_col = solve(inverse, right_col).astype(jnp.bfloat16)
    core = jnp.einsum("ktr,kts->krs", solved, solved_col, preferred_element_type=jnp.float32)
    core = core.astype(jnp.bfloat16)
    mixed = jnp.einsum("ktr,krs->kts", left, core, preferred_element_type=jnp.float32)
    mixed = mixed.astype(jnp.bfloat16)
    left_col = second.gather_end([after(part, mixed) for part in parts_two])
    change = jnp.einsum("kts,kus->tu", mixed, left_col, preferred_element_type=jnp.float32)
    return base - change


def solution(mesh):
    placed = (
        P("row", "col"),
        P("row", "col", None, None),
        P("row", "col", None, None),
        P("col", None, None),
        P("row", "col"),
        P(),
    )
    step = functools.partial(local, mesh.shape["col"], mesh.shape["row"])
    return jax.shard_map(
        step, mesh=mesh, in_specs=placed, out_specs=P("row", "col"), check_vma=False
    )
```

```python
import functools

import jax
import jax.numpy as jnp
from jax import lax
from jax.sharding import PartitionSpec as P

LOW = 2
FAN = ((1, 1), (2, 2), (3, 3))
BACK = ((2, 2), (1, 1), (3, 3))
BACK_LEFT = ((1, 1), (2, 2), (3, 3))


def after(value, earlier):
    return lax.optimization_barrier((value, earlier))[0]


def swap_cols(block):
    return lax.ppermute(block, "col", [(0, 1), (1, 0)])


def all_panels(block, cols, col):
    if cols == 2:
        return jnp.stack([block, swap_cols(block)])
    return jnp.roll(lax.all_gather(block, "col"), -col, axis=0)


class Paths:
    def __init__(self, rows, cols, col_rows, width):
        self.rows, self.cols = rows, cols
        self.row, self.col = lax.axis_index("row"), lax.axis_index("col")
        self.odd = (self.col & 1) == 1
        self.place = self.row & ((1 << LOW) - 1)
        self.apart = jnp.broadcast_to((col_rows ^ self.row)[:, None], (cols, width))
        high = list(range(LOW, rows.bit_length() - 1))
        self.high = [(1 << even, 1 << odd) for even, odd in zip(high, high[::-1])]

    def of(self, pair):
        return jnp.where(self.odd, pair[1], pair[0])

    def cross(self, block, masks):
        rows, cols = range(self.rows), range(self.cols)
        pairs = [(i * self.cols + c, (i ^ masks[c & 1]) * self.cols + c) for i in rows for c in cols]
        return lax.ppermute(block, ("row", "col"), pairs)

    def scatter_start(self, block):
        n, height, width = block.shape
        parts = block.reshape(n, 1 << LOW, height >> LOW, width)
        part = functools.partial(lax.dynamic_index_in_dim, parts, axis=1, keepdims=False)
        sent = [part(self.place ^ self.of(masks)) for masks in FAN]
        return part(self.place), [self.cross(block, masks) for block, masks in zip(sent, FAN)], sent

    def scatter_end(self, slots, came):
        low = (self.apart & ((1 << LOW) - 1))[:, None, None, :]
        for masks, block in zip(FAN, came):
            slots = jnp.where(low == self.of(masks), block, slots)
        return slots

    def spread(self, slots, came, step):
        mine = (jnp.arange(self.cols) == self.col)[:, None]
        apart = jnp.sum(jnp.where(mine, self.apart, 0), axis=0)
        return jnp.where((apart & self.of(self.high[step])) == 0, slots, came)

    def own_columns(self, slots):
        if self.cols == 2:
            mine = jnp.where(self.col == 0, slots[0], slots[1])
            other = jnp.where(self.col == 0, slots[1], slots[0])
            return jnp.stack([mine, swap_cols(other)])
        return jnp.roll(lax.all_to_all(slots, "col", 0, 0, tiled=True), -self.col, axis=0)

    def gather_start(self, held, fan=BACK):
        return [held, *(self.cross(held, masks) for masks in fan)]

    def gather_end(self, parts, fan=BACK):
        masks = [self.of(masks) for masks in fan]
        whole = []
        for q in range(1 << LOW):
            part = parts[0]
            for mask, came in zip(masks, parts[1:]):
                part = jnp.where((self.place ^ q) == mask, came, part)
            whole.append(part)
        return jnp.concatenate(whole, axis=1)


def local(cols, rows, trailing, u_factor, w_factor, diag_inverse, ranks, col_rows):
    rank_max = w_factor.shape[3]
    col = lax.axis_index("col")
    left, inverse = u_factor[0, 0], diag_inverse[0]
    keep = jnp.arange(rank_max, dtype=jnp.int32) < ranks[0, 0]
    right = jnp.where(keep[None, :], w_factor[0, 0], jnp.zeros((), jnp.bfloat16))
    first, second = (Paths(rows, cols, c, rank_max) for c in (col_rows, after(col_rows, left)))
    both = jnp.stack([right, left])
    slots, came, sent = first.scatter_start(both)

    own = all_panels(both, cols, col)
    inverse = all_panels(after(inverse, own), cols, col)
    right, left = own[:, 0], own[:, 1]
    solve = functools.partial(jnp.einsum, "ktu,kur->ktr", preferred_element_type=jnp.float32)
    solved = solve(inverse, right).astype(jnp.bfloat16)
    base = trailing.astype(jnp.float32)

    both = first.own_columns(first.scatter_end(slots, came))
    one, two = both[:, 0], both[:, 1]
    came_one = first.cross(one, first.high[0])
    came_two = second.cross(two, second.high[0])
    last = len(first.high) - 1
    for step in range(last):
        one = first.spread(one, after(came_one, two), step)
        came_one = first.cross(one, first.high[step + 1])
        two = second.spread(two, after(came_two, one), step)
        came_two = second.cross(two, second.high[step + 1])
    one = first.spread(one, after(came_one, (two, base)), last)
    parts_one = first.gather_start(one)
    two = second.spread(two, after(came_two, (one, solved)), last)
    parts_two = second.gather_start(two, BACK_LEFT)

    right_col = first.gather_end(parts_one)
    solved_col = solve(inverse, right_col).astype(jnp.bfloat16)
    core = jnp.einsum("ktr,kts->krs", solved, solved_col, preferred_element_type=jnp.float32)
    core = core.astype(jnp.bfloat16)
    mixed = jnp.einsum("ktr,krs->kts", left, core, preferred_element_type=jnp.float32)
    mixed = mixed.astype(jnp.bfloat16)
    left_col = second.gather_end([after(part, mixed) for part in parts_two], BACK_LEFT)
    change = jnp.einsum("kts,kus->tu", mixed, left_col, preferred_element_type=jnp.float32)
    return base - change


def solution(mesh):
    placed = (
        P("row", "col"),
        P("row", "col", None, None),
        P("row", "col", None, None),
        P("col", None, None),
        P("row", "col"),
        P(),
    )
    step = functools.partial(local, mesh.shape["col"], mesh.shape["row"])
    return jax.shard_map(
        step, mesh=mesh, in_specs=placed, out_specs=P("row", "col"), check_vma=False
    )
```
